256 devices in a mesh: dp: 32 (over z, x), grp: 8 (over y, core).
Axes of the slice: x: 4, y: 4, z: 8, core: 2. Of those that a mesh axis runs over, the one named last changes fastest.
Arguments:
- grad: bfloat16 [16, 2048, 2048], P(None, 'dp'), may hold values from -81 to 81
Outputs:
- update: bfloat16 [32, 1024, 2048], P('dp', 'grp')
The draws below stay inside these ranges and needn't reach their ends.
All inputs are finite; a program needn't handle non-finite values.
Results may differ from the reference program's by a relative error of at most 0.0033.
The reference program's roundings to bfloat16 on the way count: a program that leaves them out, or rounds other values in their place, can miss the bound.
Values may be sent and summed in bfloat16 or wider, within the bound.
A program may use at most 128 MiB of HBM per device.

```python
import math
import jax
import jax.numpy as jnp
from jax import lax

B = 2048
PSTEPS = 8
BLOCKS = 16
HALF = 128


def draw_grad(key, part):
    key = jax.random.fold_in(key, 11)
    key_base, key_rows, key_cols = jax.random.split(key, 3)
    ramp = jnp.arange(B, dtype=jnp.float32) / B
    row_scale = jnp.exp(math.log(10.0) * ramp[None, :, None] + jax.random.uniform(key_rows, (BLOCKS, B, 1), jnp.float32, -0.35, 0.35))
    col_scale = jnp.exp(math.log(10.0) * ramp[None, None, :] + jax.random.uniform(key_cols, (BLOCKS, 1, B), jnp.float32, -0.35, 0.35))
    base = jnp.clip(jax.random.normal(key_base, (BLOCKS, B, B), jnp.float32), -4.0, 4.0)
    return (0.1 * base * row_scale * col_scale).astype(jnp.bfloat16)


def setup_inputs(seed: int = 0) -> dict:
    seeds = jax.random.split(jax.random.key(seed), 2)
    return {
        "grad": draw_grad(jax.random.fold_in(seeds[1], 71), 0),
    }


damping = 0.1
graft_floor = 1e-06

def matmul(left, right):
    return jnp.dot(left.astype(jnp.float32), right.astype(jnp.float32))

def factor_root(operand):
    width = operand.shape[0]
    identity = jnp.eye(width, dtype=jnp.float32)
    stat = matmul(operand, operand.T) / width + damping * identity
    vector = jnp.ones((width,), jnp.float32) / math.sqrt(width)
    norm = jnp.float32(1.0)
    for step in range(PSTEPS):
        image = jnp.dot(stat, vector, precision=lax.Precision.HIGHEST)
        norm = jnp.sqrt(jnp.sum(image * image))
        vector = image / norm
    t_zero = ((5.0 * identity - stat / norm) / 4.0).astype(jnp.bfloat16)
    square = matmul(t_zero, t_zero).astype(jnp.bfloat16)
    fourth = matmul(square, square)
    fifth = matmul(fourth.astype(jnp.bfloat16), t_zero)
    moved = 5.0 * fourth - 4.0 * fifth
    t_one = ((5.0 * identity - moved) / 4.0).astype(jnp.bfloat16)
    return matmul(t_one, t_zero).astype(jnp.bfloat16)

def refresh(block):
    left = factor_root(block)
    right = factor_root(block.T)
    mixed = matmul(left, block).astype(jnp.bfloat16)
    result = matmul(mixed, right)
    total = B * B
    grad_sq = jnp.sum(block.astype(jnp.float32) ** 2)
    upd_sq = jnp.sum(result * result)
    scaled = result * jnp.sqrt(grad_sq / total) * lax.rsqrt(upd_sq / total + graft_floor)
    scaled = scaled.astype(jnp.bfloat16)
    grouped = scaled.reshape(B // (2 * HALF), 2, HALF, B)
    return jnp.transpose(grouped, (1, 0, 2, 3)).reshape(2, B // 2, B)

def reference(grad):
    stacked = lax.map(refresh, grad)
    return stacked.reshape(2 * BLOCKS, B // 2, B)
```

```python
import functools
import math

import jax
import jax.numpy as jnp
from jax import lax
from jax.experimental import pallas as pl
from jax.experimental.pallas import tpu as pltpu
from jax.sharding import PartitionSpec as P

PSTEPS = 8
damping = 0.1
graft_floor = 1e-06

MESH = pl.DeviceIdType.MESH
f32 = jnp.float32
bf16 = jnp.bfloat16
N = 2048
TILE = 256
HALF = 128
LANES = 128
NT = (((1,), (1,)), ((), ()))
ZORDER = (0, 1, 7, 2, 6, 3, 5, 4)


def at(start, size, unit=None):
    return pl.ds(pl.multiple_of(start, unit or size), size)


def spread_kernel(grad, block, local_sem, send1, recv1, send2, recv2):
    dp = lax.axis_index("dp")
    grp = lax.axis_index("grp")
    z, x = dp // 4, lax.rem(dp, 4)
    y, core = grp // 2, lax.rem(grp, 2)
    up = lax.rem(y + 1, 4) * 2 + core
    down = lax.rem(y + 3, 4) * 2 + core
    across = lax.rem(y + 2, 4) * 2 + core
    sibling = grp + 1 - 2 * core

    def flip(g):
        return g + 1 - 2 * core

    barrier = pltpu.get_barrier_semaphore()

    def greet(k, _):
        pl.semaphore_signal(
            barrier, inc=1, device_id={"dp": lax.rem(dp + k, 32)}, device_id_type=MESH
        )
        return 0

    lax.fori_loop(1, 32, greet, 0)
    for g in (up, down, sibling):
        pl.semaphore_signal(barrier, inc=1, device_id={"grp": g}, device_id_type=MESH)
    pl.semaphore_wait(barrier, 34)

    def piece(dz, dx):
        target = lax.rem(z + dz, 8) * 4 + lax.rem(x + dx, 4)
        return pltpu.make_async_remote_copy(
            src_ref=grad.at[target // 2, :, at(grp * TILE, TILE)],
            dst_ref=block.at[at(dp * 64, 64), at(grp * TILE, TILE)],
            send_sem=send1.at[dz * 4 + dx],
            recv_sem=recv1.at[dz * 4 + dx],
            device_id={"dp": target},
            device_id_type=MESH,
        )

    own = pltpu.make_async_copy(
        grad.at[dp // 2, :, at(grp * TILE, TILE)],
        block.at[at(dp * 64, 64), at(grp * TILE, TILE)],
        local_sem,
    )
    own.start()
    for dz in ZORDER:
        for dx in range(4):
            if dz or dx:
                piece(dz, dx).start()

    def relay(q, column, target, slot):
        rows = at(lax.rem(z + 8 - ZORDER[q], 8) * TILE, TILE)
        ref = block.at[rows, at(column * TILE, TILE)]
        return pltpu.make_async_remote_copy(
            src_ref=ref,
            dst_ref=ref,
            send_sem=send2.at[slot, q],
            recv_sem=recv2.at[slot, q],
            device_id={"grp": target},
            device_id_type=MESH,
        )

    started = []

    def go(*args):
        copy = relay(*args)
        copy.start()
        started.append(copy)

    def first(q):
        for dx in range(4):
            if ZORDER[q] or dx:
                piece(ZORDER[q], dx).wait_recv()
            else:
                own.wait()
        go(q, grp, up, 0)
        go(q, grp, down, 1)
        go(q, grp, sibling, 2)

    def second(q):
        relay(q, down, up, 0).wait_recv()
        if q % 2 == 0:
            go(q, down, up, 3)
        relay(q, up, down, 1).wait_recv()
        if q % 2:
            go(q, up, down, 3)
        go(q, down, sibling, 4)
        go(q, up, sibling, 5)

    def third(q):
        relay(q, across, up, 3).wait_recv()
        go(q, across, sibling, 6)

    for q in range(8 + 2):
        if q < 8:
            first(q)
        if 1 <= q < 9:
            second(q - 1)
        if 2 <= q:
            third(q - 2)
    for q in range(8):
        relay(q, sibling, sibling, 2).wait_recv()
        relay(q, flip(down), sibling, 4).wait_recv()
        relay(q, flip(up), sibling, 5).wait_recv()
        relay(q, flip(across), sibling, 6).wait_recv()
    for copy in started:
        copy.wait_send()
    for dz in ZORDER:
        for dx in range(4):
            if dz or dx:
                piece(dz, dx).wait_send()


def spread(grad):
    return pl.pallas_call(
        spread_kernel,
        out_shape=jax.ShapeDtypeStruct((N, N), bf16),
        in_specs=[pl.BlockSpec(memory_space=pl.ANY)],
        out_specs=pl.BlockSpec(memory_space=pl.ANY),
        scratch_shapes=[
            pltpu.SemaphoreType.DMA,
            pltpu.SemaphoreType.DMA((32,)),
            pltpu.SemaphoreType.DMA((32,)),
            pltpu.SemaphoreType.DMA((7, 8)),
            pltpu.SemaphoreType.DMA((7, 8)),
        ],
        compiler_params=pltpu.CompilerParams(collective_id=0, has_side_effects=True),
    )(grad)


def transpose_into(source, target):
    def step(k, _):
        i, j = k // 8, lax.rem(k, 8)
        target[at(j * TILE, TILE), at(i * TILE, TILE)] = source[
            at(i * TILE, TILE), at(j * TILE, TILE)
        ].T
        return 0

    lax.fori_loop(0, 64, step, 0)


def gram(operand, stat):
    def tile(i, distance):
        j = lax.rem(i + distance, 8)
        rows, columns = at(i * TILE, TILE), at(j * TILE, TILE)
        value = lax.dot_general(
            operand[rows, :], operand[columns, :], NT, preferred_element_type=f32
        ) * (1.0 / N)
        stat[rows, columns] = value
        if distance in (1, 2, 3):
            stat[columns, rows] = value.T

    def row(i, _):
        for distance in range(5):
            tile(i, distance)
        return 0

    lax.fori_loop(0, 8, row, 0)


def eye(size):
    return lax.broadcasted_iota(jnp.int32, (size, size), 0) == lax.broadcasted_iota(
        jnp.int32, (size, size), 1
    )


def add_diagonal(stat, value):
    def step(i, trace):
        where = (at(i * TILE, TILE), at(i * TILE, TILE))
        old, mask = stat[where], eye(TILE)
        stat[where] = jnp.where(mask, old + value, old)
        return trace + jnp.sum(jnp.where(mask, old, 0.0), keepdims=True)

    return lax.fori_loop(0, 8, step, jnp.zeros((1, 1), f32))


def fold(value):
    parts = value.reshape(value.shape[0] // 8, 8, LANES)
    total = parts[0]
    for q in range(1, parts.shape[0]):
        total = total + parts[q]
    return total


def power(stat, rows=128):
    count = N // LANES
    blocks = N // rows

    def images(i, vector):
        where = at(i * rows, rows)
        total = stat[where, 0:LANES] * vector[0][:1]
        for k in range(1, count):
            total = total + stat[where, k * LANES : (k + 1) * LANES] * vector[k][:1]
        return jnp.sum(total, axis=1, keepdims=True)

    def shares(i, image, sums):
        where = at(i * rows, rows)
        return tuple(
            sums[k] + fold(stat[where, k * LANES : (k + 1) * LANES] * image)
            for k in range(count)
        )

    def double(_, carry):
        vector, _norm = carry

        def body(i, state):
            image, sums, squares = state
            later = images(i + 1, vector)
            return later, shares(i, image, sums), squares + image * image

        image, sums, squares = lax.fori_loop(
            0,
            blocks - 1,
            body,
            (
                images(0, vector),
                tuple(jnp.zeros((8, LANES), f32) for _ in range(count)),
                jnp.zeros((rows, 1), f32),
            ),
        )
        sums = shares(blocks - 1, image, sums)
        first = jnp.sum(squares + image * image, axis=0, keepdims=True)
        result = [jnp.sum(s, axis=0, keepdims=True) for s in sums]
        square = result[0] * result[0]
        for k in range(1, count):
            square = square + result[k] * result[k]
        second = jnp.sum(square, axis=1, keepdims=True)
        norm = jnp.sqrt(second) / jnp.sqrt(first)
        inverse = 1.0 / jnp.sqrt(second)
        return tuple(jnp.broadcast_to(r * inverse, (8, LANES)) for r in result), norm

    start = tuple(jnp.full((8, LANES), 1.0 / math.sqrt(N), f32) for _ in range(count))
    return lax.fori_loop(0, PSTEPS // 2, double, (start, jnp.ones((1, 1), f32)))[1]


def build(stat, norm, near, rows=128):
    scale = -0.25 / norm
    count = N // LANES

    def body(i, sums):
        where = at(i * rows, rows)
        out = []
        for k in range(count):
            columns = slice(k * LANES, (k + 1) * LANES)
            value = (stat[where, columns] * scale).astype(bf16)
            near[where, columns] = value
            wide = value.astype(f32)
            out.append(sums[k] + fold(wide * wide))
        return tuple(out)

    sums = lax.fori_loop(
        0, N // rows, body, tuple(jnp.zeros((8, LANES), f32) for _ in range(count))
    )

    def shift(i, _):
        where = (at(i * TILE, TILE), at(i * TILE, TILE))
        value = near[where].astype(f32)
        near[where] = jnp.where(eye(TILE), value - 1.25, value).astype(bf16)
        return 0

    lax.fori_loop(0, 8, shift, 0)
    return [jnp.sum(s, axis=0, keepdims=True) for s in sums]


def times(left, right, finish, width=1024):
    def step(j, _):
        columns = at(j * width, width)
        finish(columns, jnp.dot(left[...], right[:, columns], preferred_element_type=f32))
        return 0

    lax.fori_loop(0, N // width, step, 0)


def rounding(value):
    return value.astype(bf16).astype(f32) - value


def refresh_kernel(
    block,
    update,
    whole,
    near,
    stat,
    wide,
    h0,
    h1,
    h2,
    mixed,
    square_diag,
    delta,
    diags,
    totals,
    load_sem,
    mixed_sem,
    diag_send,
    diag_recv,
    total_send,
    total_recv,
    out_sem,
):
    dp = lax.axis_index("dp")
    grp = lax.axis_index("grp")
    y, core = grp // 2, lax.rem(grp, 2)
    side = lax.rem(dp, 2)
    pair = dp + 1 - 2 * side
    sibling = grp + 1 - 2 * core
    starts = (HALF * (4 * y + side), HALF * (4 * y + side + 2))

    load = pltpu.make_async_copy(block, whole, load_sem)
    load.start()
    peers = []
    for k in range(1, 8):
        d, s = k // 4, k % 4
        peers.append(
            {"dp": pair if d else dp, "grp": lax.rem(y + s, 4) * 2 + core}
        )
    barrier = pltpu.get_barrier_semaphore()
    for peer in peers + [{"grp": sibling}]:
        pl.semaphore_signal(barrier, inc=1, device_id=peer, device_id_type=MESH)
    pl.semaphore_wait(barrier, 8)
    load.wait()

    @pl.when(core == 0)
    def _():
        gram(whole, stat)

    @pl.when(core == 1)
    def _():
        transpose_into(whole, near)
        gram(near, stat)

    trace = add_diagonal(stat, damping)
    norm = power(stat)
    add_diagonal(stat, -5.0 * norm)
    square = build(stat, norm, near)
    b0, b1 = stat.at[0:TILE], stat.at[TILE : 2 * TILE]
    for k in range(N // LANES):
        square_diag[0:1, k * LANES : (k + 1) * LANES] = rounding(square[k])
    delta[...] = jnp.zeros_like(delta)

    tiles = [(at(HALF * i, HALF), at(starts[i], HALF)) for i in range(2)]
    mask = eye(HALF)

    for rows, columns in tiles:
        h0[rows, :] = near[columns, :]
        value = near[columns, columns].astype(f32)
        h0[rows, columns] = jnp.where(mask, value + 1.25, value).astype(bf16)

    def finish_q(s, value):
        h1[:, s] = (value + 1.25 * h0[:, s].astype(f32)).astype(bf16)

    times(h0, near, finish_q)

    def finish_a(s, value):
        value = value + 1.25 * h1[:, s].astype(f32)
        b0[:, s] = value
        h0[:, s] = value.astype(bf16)

    times(h1, near, finish_a)
    middle = []
    for rows, columns in tiles:
        value = b0[rows, columns]
        middle.append(jnp.sum(jnp.where(mask, value, 0.0), axis=1, keepdims=True))
        h0[rows, columns] = jnp.where(mask, 0.0, value).astype(bf16)
    for i, (rows, columns) in enumerate(tiles):
        wide[rows, :] = jnp.broadcast_to(middle[i], (HALF, LANES))

    def finish_p4(s, value):
        for i, (rows, columns) in enumerate(tiles):
            part = (
                value[HALF * i : HALF * (i + 1)]
                + 1.25 * b0[rows, s]
                + wide[rows, 0:1] * near[columns, s].astype(f32)
                + h1[rows, s].astype(f32) * square_diag[0:1, s]
            )
            b1[rows, s] = part
            h2[rows, s] = part.astype(bf16)

    times(h0, near, finish_p4)

    def row_of(values):
        return jnp.sum(jnp.where(mask, values, 0.0), axis=0, keepdims=True)

    for i, (rows, columns) in enumerate(tiles):
        delta[i, 0:1, :] = row_of(rounding(b1[rows, columns]))

    def finish_t1(s, value):
        fifth = value + 1.25 * h2[:, s].astype(f32)
        value = fifth - 1.25 * b1[:, s]
        b0[:, s] = value
        h0[:, s] = value.astype(bf16)

    times(h2, near, finish_t1)
    for i, (rows, columns) in enumerate(tiles):
        value = b0[rows, columns]
        value = jnp.where(mask, value + 1.25, value)
        h0[rows, columns] = value.astype(bf16)
        delta[i, 1:2, :] = row_of(rounding(value))

    def finish_x(s, value):
        value = value + 1.25 * h0[:, s].astype(f32)
        b1[:, s] = value
        h1[:, s] = value.astype(bf16)

    times(h0, near, finish_x)
    for i, (rows, columns) in enumerate(tiles):
        delta[i, 2:3, :] = row_of(rounding(b1[rows, columns]))

    def mixed_copy():
        return pltpu.make_async_remote_copy(
            src_ref=h2,
            dst_ref=mixed,
            send_sem=mixed_sem.at[0],
            recv_sem=mixed_sem.at[1],
            device_id={"grp": sibling},
            device_id_type=MESH,
        )

    def result_copy():
        return pltpu.make_async_remote_copy(
            src_ref=h0.at[0:HALF],
            dst_ref=update.at[0],
            send_sem=out_sem.at[0],
            recv_sem=out_sem.at[1],
            device_id={"grp": sibling},
            device_id_type=MESH,
        )

    @pl.when(core == 0)
    def _():
        def finish_y(s, value):
            h2[:, s] = value.astype(bf16)

        times(h1, whole, finish_y)
        mixed_copy().start()
        mixed_copy().wait_send()
        result_copy().wait_recv()

    @pl.when(core == 1)
    def _():
        copies = []
        for k, peer in enumerate(peers):
            for i, (rows, columns) in enumerate(tiles):
                copies.append(
                    pltpu.make_async_remote_copy(
                        src_ref=delta.at[i],
                        dst_ref=diags.at[:, columns],
                        send_sem=diag_send.at[k, i],
                        recv_sem=diag_recv.at[k, i],
                        device_id=peer,
                        device_id_type=MESH,
                    )
                )
        for copy in copies:
            copy.start()
        for i, (rows, columns) in enumerate(tiles):
            diags[:, columns] = delta[i]
        for copy in copies:
            copy.wait()
        mixed_copy().wait_recv()

        def y_of(s):
            return mixed[:, s].astype(f32)

        def finish_1(s, value):
            value = value + 1.25 * y_of(s)
            b0[:, s] = value
            h0[:, s] = value.astype(bf16)

        times(mixed, near, finish_1)

        def finish_2(s, value):
            value = value + 1.25 * b0[:, s] + y_of(s) * square_diag[0:1, s]
            b1[:, s] = value
            h2[:, s] = value.astype(bf16)

        times(h0, near, finish_2)

        def finish_3(s, value):
            value = value + 1.25 * b1[:, s]
            b0[:, s] = value
            h0[:, s] = value.astype(bf16)

        times(h2, near, finish_3)

        def finish_4(s, value):
            value = value + 1.25 * b0[:, s] + b1[:, s] * square_diag[0:1, s]
            b0[:, s] = value
            h2[:, s] = (value + y_of(s) * diags[0:1, s]).astype(bf16)

        times(h0, near, finish_4)

        def finish_5(s, value):
            fourth, mix = b0[:, s], y_of(s)
            fifth = value + 1.25 * (fourth + mix * diags[0:1, s])
            value = 1.25 * (mix - fourth) + fifth + mix * diags[1:2, s]
            b1[:, s] = value
            h0[:, s] = value.astype(bf16)

        times(h2, near, finish_5)

        def finish_6(s, value):
            b0[:, s] = value + 1.25 * b1[:, s] + y_of(s) * diags[2:3, s]

        times(h0, near, finish_6)

        def squares(k, total):
            value = b0[:, at(k * LANES, LANES)]
            return total + fold(value * value)

        partial = lax.fori_loop(0, N // LANES, squares, jnp.zeros((8, LANES), f32))
        totals[0] = partial
        copies = []
        for k, peer in enumerate(peers):
            copies.append(
                pltpu.make_async_remote_copy(
                    src_ref=totals.at[0],
                    dst_ref=totals.at[k + 1],
                    send_sem=total_send.at[k],
                    recv_sem=total_recv.at[k],
                    device_id=peer,
                    device_id_type=MESH,
                )
            )
        for copy in copies:
            copy.start()
        for copy in copies:
            copy.wait()
        total = totals[0]
        for k in range(1, 8):
            total = total + totals[k]
        upd = jnp.sum(jnp.sum(total, axis=0, keepdims=True), axis=1, keepdims=True)
        factor = jnp.sqrt(trace / N) * lax.rsqrt(upd / (N * N) + graft_floor)

        def scaled(k, _):
            s = at(k * TILE, TILE)
            h0[:, s] = (b0[:, s] * factor).astype(bf16)
            return 0

        lax.fori_loop(0, N // TILE, scaled, 0)
        result_copy().start()
        keep = pltpu.make_async_copy(h0.at[HALF:TILE], update.at[0], load_sem)
        keep.start()
        keep.wait()
        result_copy().wait_send()


def refresh(block):
    return pl.pallas_call(
        refresh_kernel,
        out_shape=jax.ShapeDtypeStruct((1, HALF, N), bf16),
        in_specs=[pl.BlockSpec(memory_space=pl.ANY)],
        out_specs=pl.BlockSpec(memory_space=pl.ANY),
        scratch_shapes=[
            pltpu.VMEM((N, N), bf16),
            pltpu.VMEM((N, N), bf16),
            pltpu.VMEM((N, N), f32),
            pltpu.VMEM((TILE, LANES), f32),
            pltpu.VMEM((TILE, N), bf16),
            pltpu.VMEM((TILE, N), bf16),
            pltpu.VMEM((TILE, N), bf16),
            pltpu.VMEM((TILE, N), bf16),
            pltpu.VMEM((8, N), f32),
            pltpu.VMEM((2, 8, LANES), f32),
            pltpu.VMEM((8, N), f32),
            pltpu.VMEM((8, 8, LANES), f32),
            pltpu.SemaphoreType.DMA,
            pltpu.SemaphoreType.DMA((2,)),
            pltpu.SemaphoreType.DMA((7, 2)),
            pltpu.SemaphoreType.DMA((7, 2)),
            pltpu.SemaphoreType.DMA((7,)),
            pltpu.SemaphoreType.DMA((7,)),
            pltpu.SemaphoreType.DMA((2,)),
        ],
        compiler_params=pltpu.CompilerParams(
            collective_id=1, has_side_effects=True, vmem_limit_bytes=62 * 1024 * 1024
        ),
    )(block)


def per_device(grad):
    return refresh(spread(grad))


def solution(mesh):
    return jax.shard_map(
        per_device,
        mesh=mesh,
        in_specs=(P(None, "dp", None),),
        out_specs=P("dp", "grp", None),
        check_vma=False,
    )
```

```python
import math

import jax
import jax.numpy as jnp
from jax import lax
from jax.experimental import pallas as pl
from jax.experimental.pallas import tpu as pltpu
from jax.sharding import PartitionSpec as P

PSTEPS = 8
damping = 0.1
graft_floor = 1e-06

MESH = pl.DeviceIdType.MESH
f32 = jnp.float32
bf16 = jnp.bfloat16
N = 2048
TILE = 256
HALF = 128
LANES = 128
NT = (((1,), (1,)), ((), ()))
ZORDER = (0, 1, 7, 2, 6, 3, 5, 4)


def at(start, size, unit=None):
    return pl.ds(pl.multiple_of(start, unit or size), size)


def tile_of(block):
    return slice(block * TILE, (block + 1) * TILE)


def gram_rows(whole, stat, last):
    new = tile_of(last)

    def tile(i, _):
        rows = at(i * TILE, TILE)
        value = lax.dot_general(
            whole[rows, :], whole[new, :], NT, preferred_element_type=f32
        )
        stat[rows, new] = value
        stat[new, rows] = value.T
        return 0

    lax.fori_loop(0, last + 1, tile, 0)


def gram_depth(turned, stat, step):
    depth = slice(step * 512, (step + 1) * 512)

    def tile(i, distance):
        j = lax.rem(i + distance, 8)
        rows, columns = at(i * TILE, TILE), at(j * TILE, TILE)
        value = lax.dot_general(
            turned[rows, depth], turned[columns, depth], NT, preferred_element_type=f32
        )
        if step:
            value = value + stat[rows, columns]
        stat[rows, columns] = value
        if distance and step == 3:
            stat[columns, rows] = value.T

    def row(i, _):
        for distance in range(4):
            tile(i, distance)
        return 0

    lax.fori_loop(0, 8, row, 0)

    def opposite(i, _):
        tile(i, 4)
        return 0

    lax.fori_loop(0, 4, opposite, 0)


def turn(whole, turned, group):
    rows = tile_of(group)

    def step(j, _):
        columns = at(j * TILE, TILE)
        turned[columns, rows] = whole[rows, columns].T
        return 0

    lax.fori_loop(0, 8, step, 0)


def eye(size):
    return lax.broadcasted_iota(jnp.int32, (size, size), 0) == lax.broadcasted_iota(
        jnp.int32, (size, size), 1
    )


def add_diagonal(stat, value):
    def step(i, trace):
        where = (at(i * TILE, TILE), at(i * TILE, TILE))
        old, mask = stat[where], eye(TILE)
        stat[where] = jnp.where(mask, old + value, old)
        return trace + jnp.sum(jnp.where(mask, old, 0.0), keepdims=True)

    return lax.fori_loop(0, 8, step, jnp.zeros((1, 1), f32))


def fold(value):
    parts = value.reshape(value.shape[0] // 8, 8, LANES)
    total = parts[0]
    for q in range(1, parts.shape[0]):
        total = total + parts[q]
    return total


def power(stat, rows=128):
    count = N // LANES
    blocks = N // rows

    def images(i, vector):
        where = at(i * rows, rows)
        total = None
        for k in range(count):
            part = stat[where, k * LANES : (k + 1) * LANES].reshape(rows // 8, 8, LANES)
            part = part * vector[k][None]
            total = part if total is None else total + part
        total = jnp.sum(total.reshape(rows, LANES), axis=1, keepdims=True)
        return jnp.broadcast_to(total, (rows, LANES))

    def shares(i, image, sums):
        where = at(i * rows, rows)
        return tuple(
            sums[k] + fold(stat[where, k * LANES : (k + 1) * LANES] * image)
            for k in range(count)
        )

    def double(_, carry):
        vector, _norm = carry

        def body(i, state):
            image, sums, squares = state
            later = images(i + 1, vector)
            return later, shares(i, image, sums), squares + image * image

        image, sums, squares = lax.fori_loop(
            0,
            blocks - 1,
            body,
            (
                images(0, vector),
                tuple(jnp.zeros((8, LANES), f32) for _ in range(count)),
                jnp.zeros((rows, LANES), f32),
            ),
        )
        sums = shares(blocks - 1, image, sums)
        first = jnp.sum(squares + image * image, axis=0, keepdims=True)[:, 0:1]
        result = [jnp.sum(s, axis=0, keepdims=True) for s in sums]
        square = result[0] * result[0]
        for k in range(1, count):
            square = square + result[k] * result[k]
        second = jnp.sum(square, axis=1, keepdims=True)
        norm = jnp.sqrt(second) / jnp.sqrt(first)
        inverse = 1.0 / jnp.sqrt(second)
        return tuple(jnp.broadcast_to(r * inverse, (8, LANES)) for r in result), norm

    start = tuple(jnp.full((8, LANES), 1.0 / math.sqrt(N), f32) for _ in range(count))
    return lax.fori_loop(0, PSTEPS // 2, double, (start, jnp.ones((1, 1), f32)))[1]


def build(stat, norm, near, rows=128):
    scale = -0.25 / norm
    count = N // LANES

    def body(i, sums):
        where = at(i * rows, rows)
        out = []
        for k in range(count):
            columns = slice(k * LANES, (k + 1) * LANES)
            value = stat[where, columns] * scale
            near[where, columns] = value.astype(bf16)
            out.append(sums[k] + fold(value * value))
        return tuple(out)

    sums = lax.fori_loop(
        0, N // rows, body, tuple(jnp.zeros((8, LANES), f32) for _ in range(count))
    )
    diagonal = []
    for k in range(count):
        where = (slice(k * LANES, (k + 1) * LANES),) * 2
        plain = stat[where] * scale
        entry = (plain + 1.25).astype(bf16).astype(f32)
        near[where] = jnp.where(eye(LANES), entry - 1.25, plain).astype(bf16)
        extra = jnp.where(eye(LANES), entry * entry - plain * plain, 0.0)
        diagonal.append(jnp.sum(sums[k] + fold(extra), axis=0, keepdims=True))
    return diagonal


def times(left, right, finish, width=1024):
    def step(j, _):
        columns = at(j * width, width)
        finish(columns, jnp.dot(left[...], right[:, columns], preferred_element_type=f32))
        return 0

    lax.fori_loop(0, N // width, step, 0)


def rounding(value):
    return value.astype(bf16).astype(f32) - value


def refresh_kernel(
    grad,
    update,
    whole,
    near,
    stat,
    staging,
    wide,
    h0,
    h1,
    h2,
    mixed,
    square_diag,
    delta,
    diags,
    totals,
    local_sem,
    z_send,
    z_recv,
    x_send,
    x_recv,
    y_send,
    y_recv,
    s_send,
    s_recv,
    mixed_sem,
    diag_send,
    diag_recv,
    total_send,
    total_recv,
    out_sem,
):
    dp = lax.axis_index("dp")
    grp = lax.axis_index("grp")
    z, x = dp // 4, lax.rem(dp, 4)
    y, core = grp // 2, lax.rem(grp, 2)
    side, half = lax.rem(x, 2), x // 2
    pair = dp + 1 - 2 * side
    sibling = grp + 1 - 2 * core
    up = lax.rem(y + 1, 4) * 2 + core
    down = lax.rem(y + 3, 4) * 2 + core
    parity = lax.rem(y, 2)
    chunk = parity * 2 + core
    other_chunk = (1 - parity) * 2 + core

    peers = []
    for k in range(1, 8):
        d, s = k // 4, k % 4
        peers.append({"dp": pair if d else dp, "grp": lax.rem(y + s, 4) * 2 + core})
    crossing = [
        {"dp": z * 4 + 2 * (1 - half) + side},
        {"dp": z * 4 + 2 * (1 - half) + 1 - side},
    ]
    along = [{"dp": lax.rem(z + dz, 8) * 4 + x} for dz in ZORDER]
    greeted = along[1:] + crossing + peers + [{"grp": sibling}]
    barrier = pltpu.get_barrier_semaphore()
    for device in greeted:
        pl.semaphore_signal(barrier, inc=1, device_id=device, device_id_type=MESH)
    pl.semaphore_wait(barrier, len(greeted))

    def remote(src, dst, send, recv, device):
        return pltpu.make_async_remote_copy(
            src_ref=src,
            dst_ref=dst,
            send_sem=send,
            recv_sem=recv,
            device_id=device,
            device_id_type=MESH,
        )

    own_columns = at(chunk * 512, 512)

    def piece(q):
        return whole.at[at(q * TILE + x * 64, 64), own_columns]

    def block_of(q, same):
        first = 2 * lax.rem(z + ZORDER[q], 8)
        return grad.at[first + (half if same else 1 - half), :, own_columns]

    def z_copies(q):
        if q == 0:
            return [
                pltpu.make_async_copy(block_of(0, True), piece(0), local_sem.at[0]),
                pltpu.make_async_copy(block_of(0, False), staging.at[0], local_sem.at[1]),
            ]
        return [
            remote(block_of(q, True), piece(q), z_send.at[0, q], z_recv.at[0, q], along[q]),
            remote(
                block_of(q, False), staging.at[q], z_send.at[1, q], z_recv.at[1, q], along[q]
            ),
        ]

    def x_copies(q):
        copies = [remote(piece(q), piece(q), x_send.at[0, q], x_recv.at[0, q], {"dp": pair})]
        for i, device in enumerate(crossing):
            copies.append(
                remote(
                    staging.at[q], piece(q), x_send.at[i + 1, q], x_recv.at[i + 1, q], device
                )
            )
        return copies

    def part(q, which, i):
        return whole.at[tile_of(q), at(which * 512 + i * TILE, TILE)]

    def y_copies(q):
        return [
            remote(
                part(q, chunk, i),
                part(q, chunk, i),
                y_send.at[i, q],
                y_recv.at[i, q],
                {"grp": device},
            )
            for i, device in enumerate((up, down))
        ]

    def s_copy(q, i):
        ref = part(q, other_chunk, i - 1) if i else whole.at[tile_of(q), own_columns]
        return remote(ref, ref, s_send.at[i, q], s_recv.at[i, q], {"grp": sibling})

    for q in range(8):
        for copy in z_copies(q):
            copy.start()

    def spread_x(q):
        for copy in z_copies(q):
            if q:
                copy.wait_recv()
            else:
                copy.wait()
        for copy in x_copies(q):
            copy.start()

    def spread_y(q):
        for copy in x_copies(q):
            copy.wait_recv()
        for copy in y_copies(q):
            copy.start()
        s_copy(q, 0).start()

    def spread_s(q):
        for i, copy in enumerate(y_copies(q)):
            copy.wait_recv()
            s_copy(q, i + 1).start()

    def use(q):
        for i in range(3):
            s_copy(q, i).wait_recv()

        @pl.when(core == 0)
        def _():
            gram_rows(whole, stat, q)

        @pl.when(core == 1)
        def _():
            turn(whole, near, q)
            if q % 2:
                gram_depth(near, stat, q // 2)

    for step in range(8 + 3):
        for lag, stage in enumerate((spread_x, spread_y, spread_s, use)):
            if 0 <= step - lag < 8:
                stage(step - lag)

    for q in range(8):
        for copy in (z_copies(q) if q else []) + x_copies(q) + y_copies(q):
            copy.wait_send()
        for i in range(3):
            s_copy(q, i).wait_send()

    def position(group):
        distance = lax.rem(z + 8 - group // 2, 8)
        place = jnp.where(
            distance == 0, 0, jnp.where(distance <= 4, 2 * distance - 1, 16 - 2 * distance)
        )
        return HALF * jnp.where(core == 0, 2 * place + lax.rem(group, 2), group)

    starts = (position(4 * y + side), position(4 * y + side + 2))

    trace = add_diagonal(stat, N * damping)
    norm = power(stat)
    square = build(stat, norm, near)
    b0, b1 = stat.at[0:TILE], stat.at[TILE : 2 * TILE]
    for k in range(N // LANES):
        square_diag[0:1, k * LANES : (k + 1) * LANES] = rounding(square[k])
    delta[...] = jnp.zeros_like(delta)

    tiles = [(at(HALF * i, HALF), at(starts[i], HALF)) for i in range(2)]
    mask = eye(HALF)

    for rows, columns in tiles:
        h0[rows, :] = near[columns, :]
        value = near[columns, columns].astype(f32)
        h0[rows, columns] = jnp.where(mask, value + 1.25, value).astype(bf16)

    def finish_q(s, value):
        h1[:, s] = (value + 1.25 * h0[:, s].astype(f32)).astype(bf16)

    times(h0, near, finish_q)

    def finish_a(s, value):
        value = value + 1.25 * h1[:, s].astype(f32)
        b0[:, s] = value
        h0[:, s] = value.astype(bf16)

    times(h1, near, finish_a)
    middle = []
    for rows, columns in tiles:
        value = b0[rows, columns]
        middle.append(jnp.sum(jnp.where(mask, value, 0.0), axis=1, keepdims=True))
        h0[rows, columns] = jnp.where(mask, 0.0, value).astype(bf16)
    for i, (rows, columns) in enumerate(tiles):
        wide[rows, :] = jnp.broadcast_to(middle[i], (HALF, LANES))

    def finish_p4(s, value):
        for i, (rows, columns) in enumerate(tiles):
            part = (
                value[HALF * i : HALF * (i + 1)]
                + 1.25 * b0[rows, s]
                + wide[rows, 0:1] * near[columns, s].astype(f32)
                + h1[rows, s].astype(f32) * square_diag[0:1, s]
            )
            b1[rows, s] = part
            h2[rows, s] = part.astype(bf16)

    times(h0, near, finish_p4)

    def row_of(values):
        return jnp.sum(jnp.where(mask, values, 0.0), axis=0, keepdims=True)

    for i, (rows, columns) in enumerate(tiles):
        delta[i, 0:1, :] = row_of(rounding(b1[rows, columns]))

    def finish_t1(s, value):
        fifth = value + 1.25 * h2[:, s].astype(f32)
        value = fifth - 1.25 * b1[:, s]
        b0[:, s] = value
        h0[:, s] = value.astype(bf16)

    times(h2, near, finish_t1)
    for i, (rows, columns) in enumerate(tiles):
        value = b0[rows, columns]
        value = jnp.where(mask, value + 1.25, value)
        h0[rows, columns] = value.astype(bf16)
        delta[i, 1:2, :] = row_of(rounding(value))

    def finish_x(s, value):
        value = value + 1.25 * h0[:, s].astype(f32)
        b1[:, s] = value
        h1[:, s] = value.astype(bf16)

    times(h0, near, finish_x)
    for i, (rows, columns) in enumerate(tiles):
        delta[i, 2:3, :] = row_of(rounding(b1[rows, columns]))

    def mixed_copy():
        return pltpu.make_async_remote_copy(
            src_ref=h2,
            dst_ref=mixed,
            send_sem=mixed_sem.at[0],
            recv_sem=mixed_sem.at[1],
            device_id={"grp": sibling},
            device_id_type=MESH,
        )

    def result_copy():
        return pltpu.make_async_remote_copy(
            src_ref=h0.at[0:HALF],
            dst_ref=update.at[0],
            send_sem=out_sem.at[0],
            recv_sem=out_sem.at[1],
            device_id={"grp": sibling},
            device_id_type=MESH,
        )

    @pl.when(core == 0)
    def _():
        def finish_y(s, value):
            h2[:, s] = value.astype(bf16)

        times(h1, whole, finish_y)
        mixed_copy().start()
        mixed_copy().wait_send()
        result_copy().wait_recv()

    @pl.when(core == 1)
    def _():
        copies = []
        for k, peer in enumerate(peers):
            for i, (rows, columns) in enumerate(tiles):
                copies.append(
                    pltpu.make_async_remote_copy(
                        src_ref=delta.at[i],
                        dst_ref=diags.at[:, columns],
                        send_sem=diag_send.at[k, i],
                        recv_sem=diag_recv.at[k, i],
                        device_id=peer,
                        device_id_type=MESH,
                    )
                )
        for copy in copies:
            copy.start()
        for i, (rows, columns) in enumerate(tiles):
            diags[:, columns] = delta[i]
        for copy in copies:
            copy.wait()
        mixed_copy().wait_recv()

        def y_of(s):
            return mixed[:, s].astype(f32)

        def finish_1(s, value):
            value = value + 1.25 * y_of(s)
            b0[:, s] = value
            h0[:, s] = value.astype(bf16)

        times(mixed, near, finish_1)

        def finish_2(s, value):
            value = value + 1.25 * b0[:, s] + y_of(s) * square_diag[0:1, s]
            b1[:, s] = value
            h2[:, s] = value.astype(bf16)

        times(h0, near, finish_2)

        def finish_3(s, value):
            value = value + 1.25 * b1[:, s]
            b0[:, s] = value
            h0[:, s] = value.astype(bf16)

        times(h2, near, finish_3)

        def finish_4(s, value):
            value = value + 1.25 * b0[:, s] + b1[:, s] * square_diag[0:1, s]
            b0[:, s] = value
            h2[:, s] = (value + y_of(s) * diags[0:1, s]).astype(bf16)

        times(h0, near, finish_4)

        def finish_5(s, value):
            fourth, mix = b0[:, s], y_of(s)
            fifth = value + 1.25 * (fourth + mix * diags[0:1, s])
            value = 1.25 * (mix - fourth) + fifth + mix * diags[1:2, s]
            b1[:, s] = value
            h0[:, s] = value.astype(bf16)

        times(h2, near, finish_5)

        def finish_6(s, value):
            b0[:, s] = value + 1.25 * b1[:, s] + y_of(s) * diags[2:3, s]

        times(h0, near, finish_6)

        def squares(k, total):
            value = b0[:, at(k * LANES, LANES)]
            return total + fold(value * value)

        partial = lax.fori_loop(0, N // LANES, squares, jnp.zeros((8, LANES), f32))
        totals[0] = partial
        copies = []
        for k, peer in enumerate(peers):
            copies.append(
                pltpu.make_async_remote_copy(
                    src_ref=totals.at[0],
                    dst_ref=totals.at[k + 1],
                    send_sem=total_send.at[k],
                    recv_sem=total_recv.at[k],
                    device_id=peer,
                    device_id_type=MESH,
                )
            )
        for copy in copies:
            copy.start()
        for copy in copies:
            copy.wait()
        total = totals[0]
        for k in range(1, 8):
            total = total + totals[k]
        upd = jnp.sum(jnp.sum(total, axis=0, keepdims=True), axis=1, keepdims=True)
        factor = jnp.sqrt(trace / (N * N)) * lax.rsqrt(upd / (N * N) + graft_floor)

        def scaled(k, _):
            s = at(k * TILE, TILE)
            h0[:, s] = (b0[:, s] * factor).astype(bf16)
            return 0

        lax.fori_loop(0, N // TILE, scaled, 0)
        result_copy().start()
        keep = pltpu.make_async_copy(h0.at[HALF:TILE], update.at[0], local_sem.at[0])
        keep.start()
        keep.wait()
        result_copy().wait_send()


def refresh(grad):
    dma = pltpu.SemaphoreType.DMA
    return pl.pallas_call(
        refresh_kernel,
        out_shape=jax.ShapeDtypeStruct((1, HALF, N), bf16),
        in_specs=[pl.BlockSpec(memory_space=pl.ANY)],
        out_specs=pl.BlockSpec(memory_space=pl.ANY),
        scratch_shapes=[
            pltpu.VMEM((N, N), bf16),
            pltpu.VMEM((N, N), bf16),
            pltpu.VMEM((N, N), f32),
            pltpu.VMEM((8, 64, 512), bf16),
            pltpu.VMEM((TILE, LANES), f32),
            pltpu.VMEM((TILE, N), bf16),
            pltpu.VMEM((TILE, N), bf16),
            pltpu.VMEM((TILE, N), bf16),
            pltpu.VMEM((TILE, N), bf16),
            pltpu.VMEM((8, N), f32),
            pltpu.VMEM((2, 8, LANES), f32),
            pltpu.VMEM((8, N), f32),
            pltpu.VMEM((8, 8, LANES), f32),
            dma((2,)),
            dma((2, 8)),
            dma((2, 8)),
            dma((3, 8)),
            dma((3, 8)),
            dma((2, 8)),
            dma((2, 8)),
            dma((3, 8)),
            dma((3, 8)),
            dma((2,)),
            dma((7, 2)),
            dma((7, 2)),
            dma((7,)),
            dma((7,)),
            dma((2,)),
        ],
        compiler_params=pltpu.CompilerParams(
            collective_id=0, has_side_effects=True, vmem_limit_bytes=62 * 1024 * 1024
        ),
    )(grad)


def solution(mesh):
    return jax.shard_map(
        refresh,
        mesh=mesh,
        in_specs=(P(None, "dp", None),),
        out_specs=P("dp", "grp", None),
        check_vma=False,
    )
```

```python
import math

import jax
import jax.numpy as jnp
from jax import lax
from jax.experimental import pallas as pl
from jax.experimental.pallas import tpu as pltpu
from jax.sharding import PartitionSpec as P

PSTEPS = 8
damping = 0.1
graft_floor = 1e-06

MESH = pl.DeviceIdType.MESH
f32 = jnp.float32
bf16 = jnp.bfloat16
N = 2048
TILE = 256
HALF = 128
LANES = 128
NT = (((1,), (1,)), ((), ()))
ZORDER = (0, 1, 7, 2, 6, 3, 5, 4)
DEPTHS = ((0, 1), (2, 3), (4, 5), (6, 7))
MIRRORED = 7
SPLIT = 1
UNITS = 8 * SPLIT
UNIT = TILE // SPLIT
SHARE = UNIT // 4
LAGS = (0, 2, 4, 6)


def at(start, size, unit=None):
    return pl.ds(pl.multiple_of(start, unit or size), size)


def tile_of(block):
    return slice(block * TILE, (block + 1) * TILE)


def gram_rows(whole, stat, last):
    new = tile_of(last)

    def tile(rows):
        value = lax.dot_general(
            whole[rows, :], whole[new, :], NT, preferred_element_type=f32
        )
        stat[rows, new] = value
        stat[new, rows] = value.T

    def double(i, _):
        tile(at(i * 512, 512))
        return 0

    lax.fori_loop(0, (last + 1) // 2, double, 0)
    if last % 2 == 0:
        tile(new)


def gram_depth(turned, stat, groups):
    depth = slice(groups[0] * TILE, (groups[-1] + 1) * TILE)

    def tile(i, distance):
        j = lax.rem(i + distance, 4)
        rows, columns = at(i * 512, 512), at(j * 512, 512)
        value = lax.dot_general(
            turned[rows, depth], turned[columns, depth], NT, preferred_element_type=f32
        )
        if groups[0]:
            value = value + stat[rows, columns]
        stat[rows, columns] = value
        if distance and groups[-1] == MIRRORED:
            stat[columns, rows] = value.T

    def row(i, _):
        for distance in range(4 if groups[-1] > MIRRORED else 2):
            tile(i, distance)
        return 0

    lax.fori_loop(0, 4, row, 0)

    if groups[-1] <= MIRRORED:
        def opposite(i, _):
            tile(i, 2)
            return 0

        lax.fori_loop(0, 2, opposite, 0)


def turn(whole, turned, group):
    rows = tile_of(group)

    def step(j, _):
        columns = at(j * TILE, TILE)
        turned[columns, rows] = whole[rows, columns].T
        return 0

    lax.fori_loop(0, 8, step, 0)


def eye(size):
    return lax.broadcasted_iota(jnp.int32, (size, size), 0) == lax.broadcasted_iota(
        jnp.int32, (size, size), 1
    )


def add_diagonal(stat, value):
    def step(i, trace):
        where = (at(i * TILE, TILE), at(i * TILE, TILE))
        old, mask = stat[where], eye(TILE)
        stat[where] = jnp.where(mask, old + value, old)
        return trace + jnp.sum(jnp.where(mask, old, 0.0), keepdims=True)

    return lax.fori_loop(0, 8, step, jnp.zeros((1, 1), f32))


def fold(value):
    parts = value.reshape(value.shape[0] // 8, 8, LANES)
    total = parts[0]
    for q in range(1, parts.shape[0]):
        total = total + parts[q]
    return total


def power(stat, rows=128):
    count = N // LANES
    blocks = N // rows

    def images(i, vector):
        where = at(i * rows, rows)
        total = None
        for k in range(count):
            part = stat[where, k * LANES : (k + 1) * LANES].reshape(rows // 8, 8, LANES)
            part = part * vector[k][None]
            total = part if total is None else total + part
        total = jnp.sum(total.reshape(rows, LANES), axis=1, keepdims=True)
        return jnp.broadcast_to(total, (rows, LANES))

    def shares(i, image, sums):
        where = at(i * rows, rows)
        return tuple(
            sums[k] + fold(stat[where, k * LANES : (k + 1) * LANES] * image)
            for k in range(count)
        )

    def double(_, carry):
        vector, _norm = carry

        def body(i, state):
            image, sums, squares = state
            later = images(i + 1, vector)
            return later, shares(i, image, sums), squares + image * image

        image, sums, squares = lax.fori_loop(
            0,
            blocks - 1,
            body,
            (
                images(0, vector),
                tuple(jnp.zeros((8, LANES), f32) for _ in range(count)),
                jnp.zeros((rows, LANES), f32),
            ),
        )
        sums = shares(blocks - 1, image, sums)
        first = jnp.sum(squares + image * image, axis=0, keepdims=True)[:, 0:1]
        result = [jnp.sum(s, axis=0, keepdims=True) for s in sums]
        square = result[0] * result[0]
        for k in range(1, count):
            square = square + result[k] * result[k]
        second = jnp.sum(square, axis=1, keepdims=True)
        norm = jnp.sqrt(second) / jnp.sqrt(first)
        inverse = 1.0 / jnp.sqrt(second)
        return tuple(jnp.broadcast_to(r * inverse, (8, LANES)) for r in result), norm

    start = tuple(jnp.full((8, LANES), 1.0 / math.sqrt(N), f32) for _ in range(count))
    return lax.fori_loop(0, PSTEPS // 2, double, (start, jnp.ones((1, 1), f32)))[1]


def build(stat, norm, near, rows=128):
    scale = -0.25 / norm
    count = N // LANES

    def body(i, sums):
        where = at(i * rows, rows)
        out = []
        for k in range(count):
            columns = slice(k * LANES, (k + 1) * LANES)
            value = stat[where, columns] * scale
            near[where, columns] = value.astype(bf16)
            out.append(sums[k] + fold(value * value))
        return tuple(out)

    sums = lax.fori_loop(
        0, N // rows, body, tuple(jnp.zeros((8, LANES), f32) for _ in range(count))
    )
    diagonal = []
    for k in range(count):
        where = (slice(k * LANES, (k + 1) * LANES),) * 2
        plain = stat[where] * scale
        entry = (plain + 1.25).astype(bf16).astype(f32)
        near[where] = jnp.where(eye(LANES), entry - 1.25, plain).astype(bf16)
        extra = jnp.where(eye(LANES), entry * entry - plain * plain, 0.0)
        diagonal.append(jnp.sum(sums[k] + fold(extra), axis=0, keepdims=True))
    return diagonal


def times(left, right, finish, width=1024):
    def step(j, _):
        columns = at(j * width, width)
        finish(columns, jnp.dot(left[...], right[:, columns], preferred_element_type=f32))
        return 0

    lax.fori_loop(0, N // width, step, 0)


def rounding(value):
    return value.astype(bf16).astype(f32) - value


def refresh_kernel(
    grad,
    update,
    whole,
    near,
    other,
    stat,
    staging,
    wide,
    rows_near,
    h0,
    h1,
    h2,
    mixed,
    square_diag,
    square_right,
    delta,
    diags,
    result,
    totals,
    local_sem,
    z_send,
    z_recv,
    x_send,
    x_recv,
    y_send,
    y_recv,
    s_send,
    s_recv,
    factor_sem,
    mixed_sem,
    diag_send,
    diag_recv,
    total_send,
    total_recv,
):
    dp = lax.axis_index("dp")
    grp = lax.axis_index("grp")
    z, x = dp // 4, lax.rem(dp, 4)
    y, core = grp // 2, lax.rem(grp, 2)
    side, half = lax.rem(x, 2), x // 2
    pair = dp + 1 - 2 * side
    sibling = grp + 1 - 2 * core
    up = lax.rem(y + 1, 4) * 2 + core
    down = lax.rem(y + 3, 4) * 2 + core
    parity = lax.rem(y, 2)
    chunk = parity * 2 + core
    other_chunk = (1 - parity) * 2 + core

    peers = []
    for k in range(1, 8):
        d, s = k // 4, k % 4
        peers.append({"dp": pair if d else dp, "grp": lax.rem(y + s, 4) * 2 + core})
    crossing = [
        {"dp": z * 4 + 2 * (1 - half) + side},
        {"dp": z * 4 + 2 * (1 - half) + 1 - side},
    ]
    along = [{"dp": lax.rem(z + dz, 8) * 4 + x} for dz in ZORDER]
    greeted = along[1:] + crossing + peers + [{"grp": sibling}]
    barrier = pltpu.get_barrier_semaphore()
    for device in greeted:
        pl.semaphore_signal(barrier, inc=1, device_id=device, device_id_type=MESH)
    pl.semaphore_wait(barrier, len(greeted))

    def remote(src, dst, send, recv, device):
        return pltpu.make_async_remote_copy(
            src_ref=src,
            dst_ref=dst,
            send_sem=send,
            recv_sem=recv,
            device_id=device,
            device_id_type=MESH,
        )

    own_columns = at(chunk * 512, 512)

    def piece(q):
        return whole.at[at(q * UNIT + x * SHARE, SHARE), own_columns]

    def block_of(q, same):
        first = 2 * lax.rem(z + ZORDER[q // SPLIT], 8)
        rows = pl.ds(q % SPLIT * SHARE, SHARE)
        return grad.at[first + (half if same else 1 - half), rows, own_columns]

    def z_copies(q):
        if q < SPLIT:
            return [
                pltpu.make_async_copy(block_of(q, True), piece(q), local_sem.at[0, q]),
                pltpu.make_async_copy(block_of(q, False), staging.at[q], local_sem.at[1, q]),
            ]
        device = along[q // SPLIT]
        return [
            remote(block_of(q, True), piece(q), z_send.at[0, q], z_recv.at[0, q], device),
            remote(block_of(q, False), staging.at[q], z_send.at[1, q], z_recv.at[1, q], device),
        ]

    def x_copies(q):
        copies = [remote(piece(q), piece(q), x_send.at[0, q], x_recv.at[0, q], {"dp": pair})]
        for i, device in enumerate(crossing):
            copies.append(
                remote(
                    staging.at[q], piece(q), x_send.at[i + 1, q], x_recv.at[i + 1, q], device
                )
            )
        return copies

    def part(q, which, i):
        return whole.at[pl.ds(q * UNIT, UNIT), at(which * 512 + i * TILE, TILE)]

    def y_copies(q):
        return [
            remote(
                part(q, chunk, i),
                part(q, chunk, i),
                y_send.at[i, q],
                y_recv.at[i, q],
                {"grp": device},
            )
            for i, device in enumerate((up, down))
        ]

    def s_copy(q, i):
        own = whole.at[pl.ds(q * UNIT, UNIT), own_columns]
        ref = part(q, other_chunk, i - 1) if i else own
        return remote(ref, ref, s_send.at[i, q], s_recv.at[i, q], {"grp": sibling})

    for q in range(UNITS):
        for copy in z_copies(q):
            copy.start()

    def spread_x(q):
        for copy in z_copies(q):
            if q >= SPLIT:
                copy.wait_recv()
            else:
                copy.wait()
        for copy in x_copies(q):
            copy.start()

    def spread_y(q):
        for copy in x_copies(q):
            copy.wait_recv()
        for copy in y_copies(q):
            copy.start()
        s_copy(q, 0).start()

    def spread_s(q):
        for i, copy in enumerate(y_copies(q)):
            copy.wait_recv()
            s_copy(q, i + 1).start()

    def use(q):
        for i in range(3):
            s_copy(q, i).wait_recv()

        group = q // SPLIT
        if (q + 1) % SPLIT:
            return

        @pl.when(core == 0)
        def _():
            gram_rows(whole, stat, group)

        @pl.when(core == 1)
        def _():
            turn(whole, near, group)
            for groups in DEPTHS:
                if group == groups[-1]:
                    gram_depth(near, stat, groups)

    for step in range(UNITS + LAGS[-1]):
        for lag, stage in zip(LAGS, (spread_x, spread_y, spread_s, use)):
            if 0 <= step - lag < UNITS:
                stage(step - lag)

    for q in range(UNITS):
        for copy in (z_copies(q) if q >= SPLIT else []) + x_copies(q) + y_copies(q):
            copy.wait_send()
        for i in range(3):
            s_copy(q, i).wait_send()

    def region(group):
        distance = lax.rem(z + 8 - group // 2, 8)
        place = jnp.where(
            distance == 0, 0, jnp.where(distance <= 4, 2 * distance - 1, 16 - 2 * distance)
        )
        return TILE * jnp.where(core == 0, place, group // 2)

    def offset(i):
        arrival = (i % 64) // SHARE * UNIT + (2 * side + i // 64) * SHARE + i % SHARE
        return jnp.where(core == 0, arrival, side * HALF + i)

    regions = (region(4 * y + side), region(4 * y + side + 2))

    trace = add_diagonal(stat, N * damping)
    norm = power(stat)
    square = build(stat, norm, near)
    b0, b1 = stat.at[0:TILE], stat.at[TILE : 2 * TILE]
    for k in range(N // LANES):
        square_diag[0:1, k * LANES : (k + 1) * LANES] = rounding(square[k])
    delta[...] = jnp.zeros_like(delta)

    tiles = [(at(HALF * i, HALF), at(regions[i], TILE)) for i in range(2)]
    entry = lax.broadcasted_iota(jnp.int32, (HALF, TILE), 0)
    mask = lax.broadcasted_iota(jnp.int32, (HALF, TILE), 1) == offset(entry)

    def factor_copies():
        return [
            remote(near, other, factor_sem.at[0], factor_sem.at[1], {"grp": sibling}),
            remote(
                square_diag, square_right, factor_sem.at[2], factor_sem.at[3], {"grp": sibling}
            ),
        ]

    def factor_keeps():
        return [
            pltpu.make_async_copy(near, other, factor_sem.at[4]),
            pltpu.make_async_copy(square_diag, square_right, factor_sem.at[5]),
        ]

    @pl.when(core == 1)
    def _():
        for copy in factor_copies() + factor_keeps():
            copy.start()

    for i, (rows, columns) in enumerate(tiles):
        for j in range(4):
            start = regions[i] + jnp.where(
                core == 0,
                (j % 2 * 32) // SHARE * UNIT + (2 * side + j // 2) * SHARE + (j % 2 * 32) % SHARE,
                side * HALF + j * 32,
            )
            into = slice(i * HALF + j * 32, i * HALF + (j + 1) * 32)
            rows_near[into, :] = near[at(start, 32), :]
        h0[rows, :] = rows_near[rows, :]
        value = rows_near[rows, columns].astype(f32)
        h0[rows, columns] = jnp.where(mask, value + 1.25, value).astype(bf16)

    def finish_q(s, value):
        h1[:, s] = (value + 1.25 * h0[:, s].astype(f32)).astype(bf16)

    times(h0, near, finish_q)

    def finish_a(s, value):
        value = value + 1.25 * h1[:, s].astype(f32)
        b0[:, s] = value
        h0[:, s] = value.astype(bf16)

    times(h1, near, finish_a)
    middle = []
    for rows, columns in tiles:
        value = b0[rows, columns]
        middle.append(jnp.sum(jnp.where(mask, value, 0.0), axis=1, keepdims=True))
        h0[rows, columns] = jnp.where(mask, 0.0, value).astype(bf16)
    for i, (rows, columns) in enumerate(tiles):
        wide[rows, :] = jnp.broadcast_to(middle[i], (HALF, LANES))

    def finish_p4(s, value):
        for i, (rows, columns) in enumerate(tiles):
            part = (
                value[HALF * i : HALF * (i + 1)]
                + 1.25 * b0[rows, s]
                + wide[rows, 0:1] * rows_near[rows, s].astype(f32)
                + h1[rows, s].astype(f32) * square_diag[0:1, s]
            )
            b1[rows, s] = part
            h2[rows, s] = part.astype(bf16)

    times(h0, near, finish_p4)

    def row_of(values):
        row = jnp.sum(jnp.where(mask, values, 0.0), axis=0, keepdims=True)
        return jnp.where(side == 0, row[:, :HALF], row[:, HALF:])

    for i, (rows, columns) in enumerate(tiles):
        delta[i, 0:1, :] = row_of(rounding(b1[rows, columns]))

    def finish_t1(s, value):
        fifth = value + 1.25 * h2[:, s].astype(f32)
        value = fifth - 1.25 * b1[:, s]
        b0[:, s] = value
        h0[:, s] = value.astype(bf16)

    times(h2, near, finish_t1)
    for i, (rows, columns) in enumerate(tiles):
        value = b0[rows, columns]
        value = jnp.where(mask, value + 1.25, value)
        h0[rows, columns] = value.astype(bf16)
        delta[i, 1:2, :] = row_of(rounding(value))

    def finish_x(s, value):
        value = value + 1.25 * h0[:, s].astype(f32)
        b1[:, s] = value
        h1[:, s] = value.astype(bf16)

    times(h0, near, finish_x)
    for i, (rows, columns) in enumerate(tiles):
        delta[i, 2:3, :] = row_of(rounding(b1[rows, columns]))

    mixed_copy = remote(
        h2.at[HALF:TILE], mixed, mixed_sem.at[0], mixed_sem.at[1], {"grp": sibling}
    )
    diags_copy = remote(diags, diags, mixed_sem.at[2], mixed_sem.at[3], {"grp": sibling})

    @pl.when(core == 0)
    def _():
        def finish_y(s, value):
            mixed[:, s] = value[:HALF].astype(bf16)
            h2[HALF:TILE, s] = value[HALF:].astype(bf16)

        times(h1, whole, finish_y)
        mixed_copy.start()
        for copy in factor_copies():
            copy.wait_recv()

    @pl.when(core == 1)
    def _():
        own = [at(HALF * (4 * y + side + 2 * i), HALF) for i in range(2)]
        copies = []
        for k, peer in enumerate(peers):
            for i, columns in enumerate(own):
                copies.append(
                    remote(
                        delta.at[i],
                        diags.at[:, columns],
                        diag_send.at[k, i],
                        diag_recv.at[k, i],
                        peer,
                    )
                )
        for copy in copies:
            copy.start()
        for i, columns in enumerate(own):
            diags[:, columns] = delta[i]
        for copy in copies:
            copy.wait()
        diags_copy.start()
        for copy in factor_keeps():
            copy.wait()
        mixed_copy.wait_recv()

    top = slice(0, HALF)
    b0, b1, h0, h2 = b0.at[top], b1.at[top], h0.at[top], h1.at[top]

    def y_of(s):
        return mixed[:, s].astype(f32)

    def finish_1(s, value):
        value = value + 1.25 * y_of(s)
        b0[:, s] = value
        h0[:, s] = value.astype(bf16)

    times(mixed, other, finish_1)

    def finish_2(s, value):
        value = value + 1.25 * b0[:, s] + y_of(s) * square_right[0:1, s]
        b1[:, s] = value
        h2[:, s] = value.astype(bf16)

    times(h0, other, finish_2)

    def finish_3(s, value):
        value = value + 1.25 * b1[:, s]
        b0[:, s] = value
        h0[:, s] = value.astype(bf16)

    times(h2, other, finish_3)

    @pl.when(core == 0)
    def _():
        diags_copy.wait_recv()

    def finish_4(s, value):
        value = value + 1.25 * b0[:, s] + b1[:, s] * square_right[0:1, s]
        b0[:, s] = value
        h2[:, s] = (value + y_of(s) * diags[0:1, s]).astype(bf16)

    times(h0, other, finish_4)

    def finish_5(s, value):
        fourth, mix = b0[:, s], y_of(s)
        fifth = value + 1.25 * (fourth + mix * diags[0:1, s])
        value = 1.25 * (mix - fourth) + fifth + mix * diags[1:2, s]
        b1[:, s] = value
        h0[:, s] = value.astype(bf16)

    times(h2, other, finish_5)

    def finish_6(s, value):
        result[:, s] = value + 1.25 * b1[:, s] + y_of(s) * diags[2:3, s]

    times(h0, other, finish_6)

    def squares(k, total):
        value = result[:, at(k * LANES, LANES)]
        return total + fold(value * value)

    totals[0] = lax.fori_loop(0, N // LANES, squares, jnp.zeros((8, LANES), f32))
    copy = remote(
        totals.at[0], totals.at[8], total_send.at[7], total_recv.at[7], {"grp": sibling}
    )
    copy.start()
    copy.wait()
    totals[9] = totals[0] + totals[8]
    copies = [
        remote(totals.at[9], totals.at[k + 1], total_send.at[k], total_recv.at[k], peer)
        for k, peer in enumerate(peers)
    ]
    for copy in copies:
        copy.start()
    for copy in copies:
        copy.wait()
    total = totals[9]
    for k in range(1, 8):
        total = total + totals[k]
    upd = jnp.sum(jnp.sum(total, axis=0, keepdims=True), axis=1, keepdims=True)
    value = jnp.sqrt(trace / (N * N)) * lax.rsqrt(upd / (N * N) + graft_floor)
    update[0] = (result[...] * value).astype(bf16)

    @pl.when(core == 0)
    def _():
        mixed_copy.wait_send()

    @pl.when(core == 1)
    def _():
        diags_copy.wait_send()
        for copy in factor_copies():
            copy.wait_send()


def refresh(grad):
    dma = pltpu.SemaphoreType.DMA
    return pl.pallas_call(
        refresh_kernel,
        out_shape=jax.ShapeDtypeStruct((1, HALF, N), bf16),
        in_specs=[pl.BlockSpec(memory_space=pl.ANY)],
        out_specs=pl.BlockSpec(memory_space=pltpu.VMEM),
        scratch_shapes=[
            pltpu.VMEM((N, N), bf16),
            pltpu.VMEM((N, N), bf16),
            pltpu.VMEM((N, N), bf16),
            pltpu.VMEM((N, N), f32),
            pltpu.VMEM((UNITS, SHARE, 512), bf16),
            pltpu.VMEM((TILE, LANES), f32),
            pltpu.VMEM((TILE, N), bf16),
            pltpu.VMEM((TILE, N), bf16),
            pltpu.VMEM((TILE, N), bf16),
            pltpu.VMEM((TILE, N), bf16),
            pltpu.VMEM((HALF, N), bf16),
            pltpu.VMEM((8, N), f32),
            pltpu.VMEM((8, N), f32),
            pltpu.VMEM((2, 8, LANES), f32),
            pltpu.VMEM((8, N), f32),
            pltpu.VMEM((HALF, N), f32),
            pltpu.VMEM((10, 8, LANES), f32),
            dma((2, SPLIT)),
            dma((2, UNITS)),
            dma((2, UNITS)),
            dma((3, UNITS)),
            dma((3, UNITS)),
            dma((2, UNITS)),
            dma((2, UNITS)),
            dma((3, UNITS)),
            dma((3, UNITS)),
            dma((6,)),
            dma((4,)),
            dma((7, 2)),
            dma((7, 2)),
            dma((8,)),
            dma((8,)),
        ],
        compiler_params=pltpu.CompilerParams(
            collective_id=0, has_side_effects=True, vmem_limit_bytes=62 * 1024 * 1024
        ),
    )(grad)

def solution(mesh):
    return jax.shard_map(
        refresh,
        mesh=mesh,
        in_specs=(P(None, "dp", None),),
        out_specs=P("dp", "grp", None),
        check_vma=False,
    )
```

```python
import math

import jax
import jax.numpy as jnp
from jax import lax
from jax.experimental import pallas as pl
from jax.experimental.pallas import tpu as pltpu
from jax.sharding import PartitionSpec as P

PSTEPS = 8
damping = 0.1
graft_floor = 1e-06

MESH = pl.DeviceIdType.MESH
f32 = jnp.float32
bf16 = jnp.bfloat16
N = 2048
TILE = 256
HALF = 128
LANES = 128
NT = (((1,), (1,)), ((), ()))
ZORDER = (0, 1, 7, 2, 6, 3, 5, 4)
DEPTHS = ((0, 1), (2, 3), (4, 5), (6, 7))
MIRRORED = 7
SPLIT = 1
UNITS = 8 * SPLIT
UNIT = TILE // SPLIT
SHARE = UNIT // 4
LAGS = (0, 2, 4, 6)


def at(start, size, unit=None):
    return pl.ds(pl.multiple_of(start, unit or size), size)


def tile_of(block):
    return slice(block * TILE, (block + 1) * TILE)


def gram_rows(whole, stat, last):
    new = tile_of(last)

    def tile(rows):
        value = lax.dot_general(
            whole[rows, :], whole[new, :], NT, preferred_element_type=f32
        )
        stat[rows, new] = value
        stat[new, rows] = value.T

    def double(i, _):
        tile(at(i * 512, 512))
        return 0

    lax.fori_loop(0, (last + 1) // 2, double, 0)
    if last % 2 == 0:
        tile(new)


def gram_depth(turned, stat, groups):
    depth = slice(groups[0] * TILE, (groups[-1] + 1) * TILE)

    def tile(i, distance):
        j = lax.rem(i + distance, 4)
        rows, columns = at(i * 512, 512), at(j * 512, 512)
        value = lax.dot_general(
            turned[rows, depth], turned[columns, depth], NT, preferred_element_type=f32
        )
        if groups[0]:
            value = value + stat[rows, columns]
        stat[rows, columns] = value
        if distance and groups[-1] == MIRRORED:
            stat[columns, rows] = value.T

    def row(i, _):
        for distance in range(4 if groups[-1] > MIRRORED else 2):
            tile(i, distance)
        return 0

    lax.fori_loop(0, 4, row, 0)

    if groups[-1] <= MIRRORED:
        def opposite(i, _):
            tile(i, 2)
            return 0

        lax.fori_loop(0, 2, opposite, 0)


def turn(whole, turned, group):
    rows = tile_of(group)

    def step(j, _):
        columns = at(j * TILE, TILE)
        turned[columns, rows] = whole[rows, columns].T
        return 0

    lax.fori_loop(0, 8, step, 0)


def eye(size):
    return lax.broadcasted_iota(jnp.int32, (size, size), 0) == lax.broadcasted_iota(
        jnp.int32, (size, size), 1
    )


def add_diagonal(stat, value):
    trace = jnp.zeros((8, LANES), f32)
    mask = eye(LANES)
    for k in range(N // LANES):
        where = (slice(k * LANES, (k + 1) * LANES),) * 2
        old = stat[where]
        stat[where] = jnp.where(mask, old + value, old)
        trace = trace + fold(jnp.where(mask, old, 0.0))
    return jnp.sum(jnp.sum(trace, axis=0, keepdims=True), axis=1, keepdims=True)


def fold(value):
    parts = value.reshape(value.shape[0] // 8, 8, LANES)
    total = parts[0]
    for q in range(1, parts.shape[0]):
        total = total + parts[q]
    return total


def power(stat, images, rows=512, part=64):
    count = N // LANES
    blocks = N // rows
    ones = jnp.ones((LANES, LANES), bf16)

    def column(k):
        return slice(k * LANES, (k + 1) * LANES)

    def image(i, vector):
        for p in range(rows // part):
            where = at(i * rows + p * part, part)
            total = None
            for k in range(count):
                value = stat[where, column(k)].reshape(part // 8, 8, LANES) * vector[k][None]
                total = value if total is None else total + value
            total = total.reshape(part, LANES)
            high = total.astype(bf16)
            low = (total - high.astype(f32)).astype(bf16)
            images[where, :] = jnp.dot(
                high, ones, preferred_element_type=f32
            ) + jnp.dot(low, ones, preferred_element_type=f32)

    def share(i, sums, squares):
        sums = list(sums)
        for p in range(rows // part):
            where = at(i * rows + p * part, part)
            entries = images[where, :]
            squares = squares + fold(entries * entries)
            for k in range(count):
                sums[k] = sums[k] + fold(stat[where, column(k)] * entries)
        return tuple(sums), squares

    def double(_, carry):
        vector, _norm = carry
        image(0, vector)

        def body(i, state):
            image(i + 1, vector)
            return share(i, *state)

        zero = jnp.zeros((8, LANES), f32)
        state = lax.fori_loop(0, blocks - 1, body, ((zero,) * count, zero))
        sums, squares = share(blocks - 1, *state)
        first = jnp.sum(squares, axis=0, keepdims=True)[:, 0:1]
        result = [jnp.sum(s, axis=0, keepdims=True) for s in sums]
        square = result[0] * result[0]
        for k in range(1, count):
            square = square + result[k] * result[k]
        second = jnp.sum(square, axis=1, keepdims=True)
        norm = jnp.sqrt(second) / jnp.sqrt(first)
        inverse = 1.0 / jnp.sqrt(second)
        return tuple(jnp.broadcast_to(r * inverse, (8, LANES)) for r in result), norm

    start = tuple(jnp.full((8, LANES), 1.0 / math.sqrt(N), f32) for _ in range(count))
    return lax.fori_loop(0, PSTEPS // 2, double, (start, jnp.ones((1, 1), f32)))[1]


def build(stat, norm, near, rows=128):
    scale = -0.25 / norm
    count = N // LANES

    def body(i, sums):
        where = at(i * rows, rows)
        out = []
        for k in range(count):
            columns = slice(k * LANES, (k + 1) * LANES)
            value = stat[where, columns] * scale
            near[where, columns] = value.astype(bf16)
            out.append(sums[k] + fold(value * value))
        return tuple(out)

    sums = lax.fori_loop(
        0, N // rows, body, tuple(jnp.zeros((8, LANES), f32) for _ in range(count))
    )
    diagonal = []
    for k in range(count):
        where = (slice(k * LANES, (k + 1) * LANES),) * 2
        plain = stat[where] * scale
        entry = (plain + 1.25).astype(bf16).astype(f32)
        near[where] = jnp.where(eye(LANES), entry - 1.25, plain).astype(bf16)
        extra = jnp.where(eye(LANES), entry * entry - plain * plain, 0.0)
        diagonal.append(jnp.sum(sums[k] + fold(extra), axis=0, keepdims=True))
    return diagonal


def times(left, right, finish, width=1024):
    def step(j, _):
        columns = at(j * width, width)
        finish(columns, jnp.dot(left[...], right[:, columns], preferred_element_type=f32))
        return 0

    lax.fori_loop(0, N // width, step, 0)


def rounding(value):
    return value.astype(bf16).astype(f32) - value


def refresh_kernel(
    grad,
    update,
    whole,
    near,
    other,
    stat,
    staging,
    images,
    wide,
    rows_near,
    h0,
    h1,
    h2,
    mixed,
    square_diag,
    square_right,
    delta,
    diags,
    result,
    totals,
    local_sem,
    z_send,
    z_recv,
    x_send,
    x_recv,
    y_send,
    y_recv,
    s_send,
    s_recv,
    factor_sem,
    mixed_sem,
    diag_send,
    diag_recv,
    total_send,
    total_recv,
):
    dp = lax.axis_index("dp")
    grp = lax.axis_index("grp")
    z, x = dp // 4, lax.rem(dp, 4)
    y, core = grp // 2, lax.rem(grp, 2)
    side, half = lax.rem(x, 2), x // 2
    pair = dp + 1 - 2 * side
    sibling = grp + 1 - 2 * core
    up = lax.rem(y + 1, 4) * 2 + core
    down = lax.rem(y + 3, 4) * 2 + core
    parity = lax.rem(y, 2)
    chunk = parity * 2 + core
    other_chunk = (1 - parity) * 2 + core

    peers = []
    for k in range(1, 8):
        d, s = k // 4, k % 4
        peers.append({"dp": pair if d else dp, "grp": lax.rem(y + s, 4) * 2 + core})
    crossing = [
        {"dp": z * 4 + 2 * (1 - half) + side},
        {"dp": z * 4 + 2 * (1 - half) + 1 - side},
    ]
    along = [{"dp": lax.rem(z + dz, 8) * 4 + x} for dz in ZORDER]
    greeted = along[1:] + crossing + peers + [{"grp": sibling}]
    barrier = pltpu.get_barrier_semaphore()
    for device in greeted:
        pl.semaphore_signal(barrier, inc=1, device_id=device, device_id_type=MESH)
    pl.semaphore_wait(barrier, len(greeted))

    def remote(src, dst, send, recv, device):
        return pltpu.make_async_remote_copy(
            src_ref=src,
            dst_ref=dst,
            send_sem=send,
            recv_sem=recv,
            device_id=device,
            device_id_type=MESH,
        )

    own_columns = at(chunk * 512, 512)

    def piece(q):
        return whole.at[at(q * UNIT + x * SHARE, SHARE), own_columns]

    def block_of(q, same):
        first = 2 * lax.rem(z + ZORDER[q // SPLIT], 8)
        rows = pl.ds(q % SPLIT * SHARE, SHARE)
        return grad.at[first + (half if same else 1 - half), rows, own_columns]

    def z_copies(q):
        if q < SPLIT:
            return [
                pltpu.make_async_copy(block_of(q, True), piece(q), local_sem.at[0, q]),
                pltpu.make_async_copy(block_of(q, False), staging.at[q], local_sem.at[1, q]),
            ]
        device = along[q // SPLIT]
        return [
            remote(block_of(q, True), piece(q), z_send.at[0, q], z_recv.at[0, q], device),
            remote(block_of(q, False), staging.at[q], z_send.at[1, q], z_recv.at[1, q], device),
        ]

    def x_copies(q):
        copies = [remote(piece(q), piece(q), x_send.at[0, q], x_recv.at[0, q], {"dp": pair})]
        for i, device in enumerate(crossing):
            copies.append(
                remote(
                    staging.at[q], piece(q), x_send.at[i + 1, q], x_recv.at[i + 1, q], device
                )
            )
        return copies

    def part(q, which, i):
        return whole.at[pl.ds(q * UNIT, UNIT), at(which * 512 + i * TILE, TILE)]

    def y_copies(q):
        return [
            remote(
                part(q, chunk, i),
                part(q, chunk, i),
                y_send.at[i, q],
                y_recv.at[i, q],
                {"grp": device},
            )
            for i, device in enumerate((up, down))
        ]

    def s_copy(q, i):
        own = whole.at[pl.ds(q * UNIT, UNIT), own_columns]
        ref = part(q, other_chunk, i - 1) if i else own
        return remote(ref, ref, s_send.at[i, q], s_recv.at[i, q], {"grp": sibling})

    for q in range(UNITS):
        for copy in z_copies(q):
            copy.start()

    def spread_x(q):
        for copy in z_copies(q):
            if q >= SPLIT:
                copy.wait_recv()
            else:
                copy.wait()
        for copy in x_copies(q):
            copy.start()

    def spread_y(q):
        for copy in x_copies(q):
            copy.wait_recv()
        for copy in y_copies(q):
            copy.start()
        s_copy(q, 0).start()

    def spread_s(q):
        for i, copy in enumerate(y_copies(q)):
            copy.wait_recv()
            s_copy(q, i + 1).start()

    def use(q):
        for i in range(3):
            s_copy(q, i).wait_recv()

        group = q // SPLIT
        if (q + 1) % SPLIT:
            return

        @pl.when(core == 0)
        def _():
            gram_rows(whole, stat, group)

        @pl.when(core == 1)
        def _():
            turn(whole, near, group)
            for groups in DEPTHS:
                if group == groups[-1]:
                    gram_depth(near, stat, groups)

    for step in range(UNITS + LAGS[-1]):
        for lag, stage in zip(LAGS, (spread_x, spread_y, spread_s, use)):
            if 0 <= step - lag < UNITS:
                stage(step - lag)

    for q in range(UNITS):
        for copy in (z_copies(q) if q >= SPLIT else []) + x_copies(q) + y_copies(q):
            copy.wait_send()
        for i in range(3):
            s_copy(q, i).wait_send()

    def region(group):
        distance = lax.rem(z + 8 - group // 2, 8)
        place = jnp.where(
            distance == 0, 0, jnp.where(distance <= 4, 2 * distance - 1, 16 - 2 * distance)
        )
        return TILE * jnp.where(core == 0, place, group // 2)

    def offset(i):
        arrival = (i % 64) // SHARE * UNIT + (2 * side + i // 64) * SHARE + i % SHARE
        return jnp.where(core == 0, arrival, side * HALF + i)

    regions = (region(4 * y + side), region(4 * y + side + 2))

    trace = add_diagonal(stat, N * damping)
    norm = power(stat, images)
    square = build(stat, norm, near)
    b0, b1 = stat.at[0:TILE], stat.at[TILE : 2 * TILE]
    for k in range(N // LANES):
        square_diag[0:1, k * LANES : (k + 1) * LANES] = rounding(square[k])
    delta[...] = jnp.zeros_like(delta)

    tiles = [(at(HALF * i, HALF), at(regions[i], TILE)) for i in range(2)]
    entry = lax.broadcasted_iota(jnp.int32, (HALF, TILE), 0)
    mask = lax.broadcasted_iota(jnp.int32, (HALF, TILE), 1) == offset(entry)

    def factor_copies():
        return [
            remote(near, other, factor_sem.at[0], factor_sem.at[1], {"grp": sibling}),
            remote(
                square_diag, square_right, factor_sem.at[2], factor_sem.at[3], {"grp": sibling}
            ),
        ]

    def factor_keeps():
        return [
            pltpu.make_async_copy(near, other, factor_sem.at[4]),
            pltpu.make_async_copy(square_diag, square_right, factor_sem.at[5]),
        ]

    @pl.when(core == 1)
    def _():
        for copy in factor_copies() + factor_keeps():
            copy.start()

    for i, (rows, columns) in enumerate(tiles):
        for j in range(4):
            start = regions[i] + jnp.where(
                core == 0,
                (j % 2 * 32) // SHARE * UNIT + (2 * side + j // 2) * SHARE + (j % 2 * 32) % SHARE,
                side * HALF + j * 32,
            )
            into = slice(i * HALF + j * 32, i * HALF + (j + 1) * 32)
            rows_near[into, :] = near[at(start, 32), :]
        h0[rows, :] = rows_near[rows, :]
        value = rows_near[rows, columns].astype(f32)
        h0[rows, columns] = jnp.where(mask, value + 1.25, value).astype(bf16)

    def finish_q(s, value):
        h1[:, s] = (value + 1.25 * h0[:, s].astype(f32)).astype(bf16)

    times(h0, near, finish_q)

    def finish_a(s, value):
        value = value + 1.25 * h1[:, s].astype(f32)
        b0[:, s] = value
        h0[:, s] = value.astype(bf16)

    times(h1, near, finish_a)
    middle = []
    for rows, columns in tiles:
        value = b0[rows, columns]
        middle.append(jnp.sum(jnp.where(mask, value, 0.0), axis=1, keepdims=True))
        h0[rows, columns] = jnp.where(mask, 0.0, value).astype(bf16)
    for i, (rows, columns) in enumerate(tiles):
        wide[rows, :] = jnp.broadcast_to(middle[i], (HALF, LANES))

    def finish_p4(s, value):
        for i, (rows, columns) in enumerate(tiles):
            part = (
                value[HALF * i : HALF * (i + 1)]
                + 1.25 * b0[rows, s]
                + wide[rows, 0:1] * rows_near[rows, s].astype(f32)
                + h1[rows, s].astype(f32) * square_diag[0:1, s]
            )
            b1[rows, s] = part
            h2[rows, s] = part.astype(bf16)

    times(h0, near, finish_p4)

    def row_of(values):
        row = jnp.sum(jnp.where(mask, values, 0.0), axis=0, keepdims=True)
        return jnp.where(side == 0, row[:, :HALF], row[:, HALF:])

    for i, (rows, columns) in enumerate(tiles):
        delta[i, 0:1, :] = row_of(rounding(b1[rows, columns]))

    def finish_t1(s, value):
        fifth = value + 1.25 * h2[:, s].astype(f32)
        value = fifth - 1.25 * b1[:, s]
        b0[:, s] = value
        h0[:, s] = value.astype(bf16)

    times(h2, near, finish_t1)
    for i, (rows, columns) in enumerate(tiles):
        value = b0[rows, columns]
        value = jnp.where(mask, value + 1.25, value)
        h0[rows, columns] = value.astype(bf16)
        delta[i, 1:2, :] = row_of(rounding(value))

    def finish_x(s, value):
        value = value + 1.25 * h0[:, s].astype(f32)
        b1[:, s] = value
        h1[:, s] = value.astype(bf16)

    times(h0, near, finish_x)
    for i, (rows, columns) in enumerate(tiles):
        delta[i, 2:3, :] = row_of(rounding(b1[rows, columns]))

    mixed_copy = remote(
        h2.at[HALF:TILE], mixed, mixed_sem.at[0], mixed_sem.at[1], {"grp": sibling}
    )
    diags_copy = remote(diags, diags, mixed_sem.at[2], mixed_sem.at[3], {"grp": sibling})

    @pl.when(core == 0)
    def _():
        def finish_y(s, value):
            mixed[:, s] = value[:HALF].astype(bf16)
            h2[HALF:TILE, s] = value[HALF:].astype(bf16)

        times(h1, whole, finish_y)
        mixed_copy.start()
        for copy in factor_copies():
            copy.wait_recv()

    @pl.when(core == 1)
    def _():
        own = [at(HALF * (4 * y + side + 2 * i), HALF) for i in range(2)]
        copies = []
        for k, peer in enumerate(peers):
            for i, columns in enumerate(own):
                copies.append(
                    remote(
                        delta.at[i],
                        diags.at[:, columns],
                        diag_send.at[k, i],
                        diag_recv.at[k, i],
                        peer,
                    )
                )
        for copy in copies:
            copy.start()
        for i, columns in enumerate(own):
            diags[:, columns] = delta[i]
        for copy in copies:
            copy.wait()
        diags_copy.start()
        for copy in factor_keeps():
            copy.wait()
        mixed_copy.wait_recv()

    top = slice(0, HALF)
    b0, b1, h0, h2 = b0.at[top], b1.at[top], h0.at[top], h1.at[top]

    def y_of(s):
        return mixed[:, s].astype(f32)

    def finish_1(s, value):
        value = value + 1.25 * y_of(s)
        b0[:, s] = value
        h0[:, s] = value.astype(bf16)

    times(mixed, other, finish_1)

    def finish_2(s, value):
        value = value + 1.25 * b0[:, s] + y_of(s) * square_right[0:1, s]
        b1[:, s] = value
        h2[:, s] = value.astype(bf16)

    times(h0, other, finish_2)

    def finish_3(s, value):
        value = value + 1.25 * b1[:, s]
        b0[:, s] = value
        h0[:, s] = value.astype(bf16)

    times(h2, other, finish_3)

    @pl.when(core == 0)
    def _():
        diags_copy.wait_recv()

    def finish_4(s, value):
        value = value + 1.25 * b0[:, s] + b1[:, s] * square_right[0:1, s]
        b0[:, s] = value
        h2[:, s] = (value + y_of(s) * diags[0:1, s]).astype(bf16)

    times(h0, other, finish_4)

    def finish_5(s, value):
        fourth, mix = b0[:, s], y_of(s)
        fifth = value + 1.25 * (fourth + mix * diags[0:1, s])
        value = 1.25 * (mix - fourth) + fifth + mix * diags[1:2, s]
        b1[:, s] = value
        h0[:, s] = value.astype(bf16)

    times(h2, other, finish_5)

    def finish_6(s, value):
        result[:, s] = value + 1.25 * b1[:, s] + y_of(s) * diags[2:3, s]

    times(h0, other, finish_6)

    def squares(k, total):
        value = result[:, at(k * LANES, LANES)]
        return total + fold(value * value)

    totals[0] = lax.fori_loop(0, N // LANES, squares, jnp.zeros((8, LANES), f32))
    copy = remote(
        totals.at[0], totals.at[8], total_send.at[7], total_recv.at[7], {"grp": sibling}
    )
    copy.start()
    copy.wait()
    totals[9] = totals[0] + totals[8]
    copies = [
        remote(totals.at[9], totals.at[k + 1], total_send.at[k], total_recv.at[k], peer)
        for k, peer in enumerate(peers)
    ]
    for copy in copies:
        copy.start()
    for copy in copies:
        copy.wait()
    total = totals[9]
    for k in range(1, 8):
        total = total + totals[k]
    upd = jnp.sum(jnp.sum(total, axis=0, keepdims=True), axis=1, keepdims=True)
    value = jnp.sqrt(trace / (N * N)) * lax.rsqrt(upd / (N * N) + graft_floor)
    update[0] = (result[...] * value).astype(bf16)

    @pl.when(core == 0)
    def _():
        mixed_copy.wait_send()

    @pl.when(core == 1)
    def _():
        diags_copy.wait_send()
        for copy in factor_copies():
            copy.wait_send()


def refresh(grad):
    dma = pltpu.SemaphoreType.DMA
    return pl.pallas_call(
        refresh_kernel,
        out_shape=jax.ShapeDtypeStruct((1, HALF, N), bf16),
        in_specs=[pl.BlockSpec(memory_space=pl.ANY)],
        out_specs=pl.BlockSpec(memory_space=pltpu.VMEM),
        scratch_shapes=[
            pltpu.VMEM((N, N), bf16),
            pltpu.VMEM((N, N), bf16),
            pltpu.VMEM((N, N), bf16),
            pltpu.VMEM((N, N), f32),
            pltpu.VMEM((UNITS, SHARE, 512), bf16),
            pltpu.VMEM((N, LANES), f32),
            pltpu.VMEM((TILE, LANES), f32),
            pltpu.VMEM((TILE, N), bf16),
            pltpu.VMEM((TILE, N), bf16),
            pltpu.VMEM((TILE, N), bf16),
            pltpu.VMEM((TILE, N), bf16),
            pltpu.VMEM((HALF, N), bf16),
            pltpu.VMEM((8, N), f32),
            pltpu.VMEM((8, N), f32),
            pltpu.VMEM((2, 8, LANES), f32),
            pltpu.VMEM((8, N), f32),
            pltpu.VMEM((HALF, N), f32),
            pltpu.VMEM((10, 8, LANES), f32),
            dma((2, SPLIT)),
            dma((2, UNITS)),
            dma((2, UNITS)),
            dma((3, UNITS)),
            dma((3, UNITS)),
            dma((2, UNITS)),
            dma((2, UNITS)),
            dma((3, UNITS)),
            dma((3, UNITS)),
            dma((6,)),
            dma((4,)),
            dma((7, 2)),
            dma((7, 2)),
            dma((8,)),
            dma((8,)),
        ],
        compiler_params=pltpu.CompilerParams(
            collective_id=0, has_side_effects=True, vmem_limit_bytes=62 * 1024 * 1024
        ),
    )(grad)

def solution(mesh):
    return jax.shard_map(
        refresh,
        mesh=mesh,
        in_specs=(P(None, "dp", None),),
        out_specs=P("dp", "grp", None),
        check_vma=False,
    )
```
